32 devices in a mesh: arc: 4 (over z), tile: 8 (over y, x, core).
Axes of the slice: x: 2, y: 2, z: 4, core: 2. Of those that a mesh axis runs over, the one named last changes fastest.
Arguments:
- design: bfloat16 [256, 128, 512], P(('arc', 'tile')), may hold values from -0.059814453 to 0.059814453
- observed: float32 [256, 128], P(('arc', 'tile')), may hold values from -6 to 6
- obs_type: int32 [256, 128], P(('arc', 'tile')), may hold values from 0 to 7
- owner_of: int32 [256, 4], P(('arc', 'tile')), may hold values from 0 to 7, all different within a row; in each aligned block of 8 rows (0 to 7, 8 to 15, ...) at most 8 rows name the same one
- sub_of: int32 [256, 4], P(('arc', 'tile')), may hold values from 0 to 11
- sigma_table: float32 [8], replicated, may hold values from 0.3 to 3
- solution: float32 [12288], P('tile'), may hold values from -6 to 6
- prior: float32 [12288, 12288], P('arc', 'tile'), may hold values from -0.6 to 0.6
Outputs:
- normal_matrix: float32 [12288, 12288], P('arc', 'tile')
- gradient: float32 [12288], P('tile')
The draws below stay inside these ranges and needn't reach their ends.
Inputs may be any that keep to these rules, and one draw needn't show every extreme that they name: `owner_of`: each block names 4 different owners. Among the 8 blocks of one device no owner is named more than 8 times, a bound that some block reaches in every draw.
All inputs are finite; a program needn't handle non-finite values.
Results may differ from the reference program's by a relative error of at most 0.006.
Values may be sent and summed in bfloat16 or wider, within the bound.
A program may use at most 256 MiB of HBM per device.

```python
import math
import jax
import jax.numpy as jnp
import numpy as np
from jax import lax

P_SIZE = 12288
TW = 128
ROWS = 128
NTYPES = 8
NB = 8
TPO = 12
CAP = 8
BLOCKS = 256
N_ARC = 4
N_TILE = 8


def touch_ends(array, stream_key, smallest, top_value):
    spot = [jax.random.randint(jax.random.fold_in(stream_key, axis), (), 0, length) for axis, length in enumerate(array.shape)]
    main_axis = array.shape.index(max(array.shape))
    next_to = spot[:main_axis] + [(spot[main_axis] + 1) % array.shape[main_axis]] + spot[main_axis + 1:]
    return array.at[tuple(spot)].set(smallest).at[tuple(next_to)].set(top_value)


def shard_levels(rng, shape, cuts, smallest, high):
    factor_of, own = 1.0, jax.random.fold_in(rng, 6)
    for position, parts in cuts:
        heights = jnp.exp(jax.random.uniform(jax.random.fold_in(own, position), (parts,), jnp.float32, smallest / len(cuts), high / len(cuts)))
        factor_of = factor_of * jnp.repeat(heights, shape[position] // parts).reshape([-1 if axis == position else 1 for axis in range(len(shape))])
    return factor_of


def shared_out(key, own, number, rows, amount, top, most, slope):
    ranking = jax.random.permutation(key, amount)
    packed, usual = shares(amount, rows * top, most, slope, True), shares(amount, rows * top, most, slope, False)
    places = jnp.arange(amount)

    def named(lengths, offset_by):
        used = int((lengths > 0).sum())
        fixed = max(1, used // 4)
        shifted = fixed + (places - fixed + offset_by * (used - fixed)) % max(1, amount - fixed)
        return jnp.zeros((amount,), jnp.int32).at[ranking[jnp.where(places < fixed, places, shifted)]].set(jnp.asarray(lengths, jnp.int32))

    lengths = jnp.where(number % 4 == 0, named(packed, number // 4), named(usual, number - number // 4 - 1))
    mixed = jax.random.permutation(jax.random.fold_in(own, 3), amount)
    donor, taker = mixed[0:amount // 2 * 2:2], mixed[1:amount // 2 * 2:2]
    margin = jnp.minimum(lengths[donor] - 1, most - lengths[taker]) // 2
    margin = jnp.where((donor == ranking[0]) | (taker == ranking[0]) | (lengths[taker] == 0), 0, jnp.maximum(margin, 0))
    shifted = jax.random.randint(jax.random.fold_in(own, 4), (amount // 2,), 0, 1 << 20) % (margin + 1)
    lengths = lengths.at[donor].add(-shifted).at[taker].add(shifted)
    members = jnp.searchsorted(jnp.cumsum(lengths), jnp.arange(rows * top), side="right").astype(jnp.int32)
    table = members.reshape(top, rows).T
    table = table[jax.random.permutation(jax.random.fold_in(own, 1), rows)]
    offset_by = jax.random.randint(jax.random.fold_in(own, 2), (rows, 1), 0, top)
    return jnp.take_along_axis(table, (jnp.arange(top)[None, :] + offset_by) % top, axis=1)


def shares(count, total, limit, skew, full):
    loads = [(1 << 20) // math.isqrt(standing ** skew) + 1 for standing in range(1, count + 1)]
    largest = limit if full else min(limit, max(-(-total // count), total * loads[0] // sum(loads)))
    least = 1 if total - largest >= count - 1 else 0
    given, spare = [largest] + [least] * (count - 1), total - largest - least * (count - 1)
    while spare > 0:
        candidates = [i for i in range(1, count) if given[i] < largest] or [i for i in range(1, count) if given[i] < limit]
        pool, remaining = sum([loads[i] for i in candidates]), spare
        for i in candidates:
            more = min(limit - given[i], max(1, remaining * loads[i] // pool), spare)
            given[i] = given[i] + more
            spare = spare - more
    return np.array(given)


def centred(rng, dims, deviation, bound, pieces=(), kind=jnp.bfloat16):
    drawn = deviation * jax.random.normal(rng, dims, jnp.float32)
    if pieces:
        drawn = drawn * shard_levels(rng, dims, pieces, -0.22, 0.18)
    return jnp.clip(drawn, -bound, bound).astype(kind)


def setup_inputs(seed: int = 0) -> dict:
    key_list = jax.random.split(jax.random.key(seed), 9)
    design = centred(key_list[0], (BLOCKS, ROWS, 4 * TW), 0.01, 0.059814453, ((0, 32),))
    observed = centred(key_list[1], (BLOCKS, ROWS), 1.0, 6.0, ((0, 32),), jnp.float32)
    obs_type = touch_ends(jax.random.randint(key_list[2], (BLOCKS, ROWS), 0, NTYPES), jax.random.fold_in(key_list[2], 1), 0, NTYPES - 1).astype(jnp.int32)
    owner_of_keys = jax.random.split(jax.random.fold_in(key_list[3], 1), BLOCKS // NB)
    owner_of_turns = jax.random.permutation(jax.random.fold_in(key_list[3], 3), BLOCKS // NB)
    owner_of = jax.vmap(lambda own, number: shared_out(jax.random.fold_in(key_list[3], 2), own, number, NB, N_TILE, 4, CAP, 2))(owner_of_keys, owner_of_turns).reshape((BLOCKS, 4))
    sub_of = touch_ends(jax.random.randint(key_list[4], (BLOCKS, 4), 0, TPO), jax.random.fold_in(key_list[4], 1), 0, TPO - 1).astype(jnp.int32)
    sigma_table = jnp.clip(jnp.exp(jax.random.uniform(key_list[5], (NTYPES,), jnp.float32, math.log(0.3), math.log(3.0))), 0.3, 3.0)
    solution = centred(key_list[6], (P_SIZE,), 1.0, 6.0, ((0, 8),), jnp.float32)
    prior = centred(key_list[7], (P_SIZE, P_SIZE), 0.1, 0.6, ((0, 4), (1, 8)), jnp.float32)
    return dict(design=design, observed=observed, obs_type=obs_type, owner_of=owner_of, sub_of=sub_of, sigma_table=sigma_table, solution=solution, prior=prior)


huber_limit = 1.345

def block_terms(design_block, observed_block, type_block, block_tiles, solution, sigma_table):
    tile_width = design_block.shape[1] // 4
    design_tiles = design_block.reshape(design_block.shape[0], 4, tile_width).astype(jnp.float32)
    touched = solution.reshape(-1, tile_width)[block_tiles]
    predicted = jnp.einsum('qlc,lc->q', design_tiles, touched, precision=lax.Precision.HIGHEST)
    residual = observed_block - predicted
    type_ids = jnp.arange(sigma_table.shape[0], dtype=jnp.int32)
    spread = lax.optimization_barrier(jnp.sum(jnp.where(type_block[:, None] == type_ids[None, :], sigma_table[None, :], 0.0), axis=1))
    scaled = jnp.abs(residual) / spread
    root_weight = jnp.sqrt(huber_limit / jnp.maximum(scaled, huber_limit)) / spread
    weighted = lax.optimization_barrier((root_weight[:, None, None] * design_tiles).astype(jnp.bfloat16)).astype(jnp.float32)
    target = lax.optimization_barrier((root_weight * residual).astype(jnp.bfloat16)).astype(jnp.float32)
    gram_tiles = jnp.einsum('qlc,qmr->lmcr', weighted, weighted, precision=lax.Precision.HIGHEST)
    pull_terms = jnp.einsum('qlc,q->lc', weighted, target, precision=lax.Precision.HIGHEST)
    return (gram_tiles, pull_terms)

def reference(design, observed, obs_type, owner_of, sub_of, sigma_table, solution, prior):
    tile_count = P_SIZE // TW
    per_owner = tile_count // N_TILE
    tile_ids = owner_of * per_owner + sub_of
    group_blocks = BLOCKS // N_ARC
    grouped = (design.reshape(N_ARC, group_blocks, ROWS, 4 * TW), observed.reshape(N_ARC, group_blocks, ROWS), obs_type.reshape(N_ARC, group_blocks, ROWS), tile_ids.reshape(N_ARC, group_blocks, 4))

    def block_step(state_pair, block_data):
        partial_value, grad_total = state_pair
        design_block, observed_block, type_block, block_tiles = block_data
        gram_tiles, pull_terms = block_terms(design_block, observed_block, type_block, block_tiles, solution, sigma_table)
        partial_value = partial_value.at[block_tiles[:, None], :, block_tiles[None, :], :].add(gram_tiles)
        grad_total = grad_total.at[block_tiles].add(pull_terms)
        return ((partial_value, grad_total), None)

    def group_step(state_pair, group_data):
        normal_total, grad_total = state_pair
        empty = jnp.zeros((tile_count, TW, tile_count, TW), jnp.float32)
        (partial_value, grad_total), unused = lax.scan(block_step, (empty, grad_total), group_data)
        rounded = lax.optimization_barrier(partial_value.astype(jnp.bfloat16)).astype(jnp.float32)
        return ((normal_total + rounded, grad_total), None)
    initial = (jnp.zeros((tile_count, TW, tile_count, TW), jnp.float32), jnp.zeros((tile_count, TW), jnp.float32))
    (normal_total, grad_total), unused = lax.scan(group_step, initial, grouped)
    return (prior + normal_total.reshape(P_SIZE, P_SIZE), grad_total.reshape(P_SIZE))
```

```python
import functools

import jax
import jax.numpy as jnp
from jax import lax
from jax.experimental import pallas as pl
from jax.experimental.pallas import tpu as pltpu
from jax.sharding import PartitionSpec as P

huber_limit = 1.345


def weigh_kernel(tile_ids, sigma, estimate, design, observed, obs_type, weighted, pull):
    blocks, _, row_width = design.shape
    tile_width = row_width // 4
    for block in range(blocks):
        rows = design[block].astype(jnp.float32)
        touched = jnp.concatenate(
            [estimate[pl.ds(tile_ids[4 * block + part], 1), :] for part in range(4)], axis=1
        )
        predicted = jnp.sum(rows * touched, axis=1, keepdims=True)
        residual = observed[:, block : block + 1] - predicted
        types = obs_type[:, block : block + 1]
        spread = jnp.zeros_like(residual)
        for code in range(sigma.shape[0]):
            spread = jnp.where(types == code, sigma[code], spread)
        scaled = jnp.abs(residual) / spread
        root_weight = jnp.sqrt(huber_limit / jnp.maximum(scaled, huber_limit)) / spread
        scaled_rows = (root_weight * rows).astype(jnp.bfloat16)
        target = (root_weight * residual).astype(jnp.bfloat16).astype(jnp.float32)
        weighted[block] = scaled_rows
        pull[block : block + 1, :] = jnp.sum(
            scaled_rows.astype(jnp.float32) * target, axis=0, keepdims=True
        )


def weigh(tile_ids, sigma, estimate, design, observed, obs_type):
    blocks, block_rows, row_width = design.shape
    smem, vmem = pl.BlockSpec(memory_space=pltpu.SMEM), pl.BlockSpec(memory_space=pltpu.VMEM)
    return pl.pallas_call(
        weigh_kernel,
        out_shape=(
            jax.ShapeDtypeStruct(design.shape, jnp.bfloat16),
            jax.ShapeDtypeStruct((blocks, row_width), jnp.float32),
        ),
        in_specs=[smem, smem, vmem, vmem, vmem, vmem],
        out_specs=(vmem, vmem),
        compiler_params=pltpu.CompilerParams(vmem_limit_bytes=16 << 20),
        name="weigh",
    )(tile_ids, sigma, estimate, design, observed.T, obs_type.T)


def gram_kernel(row_groups, table, items, pull, prior, normal, gradient, total, grad_total, sem):
    step = pl.program_id(0)
    chunk, _, row_width = items.shape
    tile_width = row_width // 4
    kept = normal.shape[0]
    load = pltpu.make_async_copy(prior, total.at[pl.ds(0, kept)], sem)

    @pl.when(step == 0)
    def _():
        load.start()
        grad_total[...] = jnp.zeros_like(grad_total)
        load.wait()

    fields = 2 + 2 * row_groups
    for item in range(chunk):
        base = (step * chunk + item) * fields

        def lanes(entry):
            return pl.ds(pl.multiple_of(table[base + entry] * tile_width, tile_width), tile_width)

        part = lanes(0)
        sub = table[base + 1]
        column = pl.ds(
            pl.multiple_of(jnp.minimum(sub, gradient.shape[0] - 1) * tile_width, tile_width),
            tile_width,
        )
        grad_total[pl.ds(sub, 1), :] += pull[pl.ds(item, 1), part]
        left = jnp.concatenate(
            [items[item, :, lanes(2 + 2 * group)] for group in range(row_groups)], axis=1
        )
        products = lax.dot_general(
            left,
            items[item, :, part],
            (((0,), (0,)), ((), ())),
            preferred_element_type=jnp.float32,
        )
        for group in range(row_groups):
            total[lanes(3 + 2 * group), column] += products[
                group * tile_width : (group + 1) * tile_width
            ]

    @pl.when(step == pl.num_programs(0) - 1)
    def _():
        store = pltpu.make_async_copy(total.at[pl.ds(0, kept)], normal, sem)
        store.start()
        gradient[...] = grad_total[: gradient.shape[0]]
        store.wait()


def gram(table, items, pull, prior, per_owner, row_groups, chunk):
    count, block_rows, row_width = items.shape
    tile_width = row_width // 4
    kept, width = prior.shape
    padded = -(-(per_owner + 1) // 8) * 8
    return pl.pallas_call(
        functools.partial(gram_kernel, row_groups),
        grid_spec=pltpu.PrefetchScalarGridSpec(
            num_scalar_prefetch=1,
            grid=(count // chunk,),
            in_specs=[
                pl.BlockSpec((chunk, block_rows, row_width), lambda step, table: (step, 0, 0)),
                pl.BlockSpec((chunk, row_width), lambda step, table: (step, 0)),
                pl.BlockSpec(memory_space=pl.ANY),
            ],
            out_specs=(
                pl.BlockSpec(memory_space=pl.ANY),
                pl.BlockSpec((per_owner, tile_width), lambda step, table: (0, 0)),
            ),
            scratch_shapes=[
                pltpu.VMEM((kept + tile_width, width), jnp.float32),
                pltpu.VMEM((padded, tile_width), jnp.float32),
                pltpu.SemaphoreType.DMA,
            ],
        ),
        out_shape=(
            jax.ShapeDtypeStruct(prior.shape, jnp.float32),
            jax.ShapeDtypeStruct((per_owner, tile_width), jnp.float32),
        ),
        compiler_params=pltpu.CompilerParams(
            vmem_limit_bytes=(kept + tile_width) * width * 4 + (12 << 20)
        ),
        name="gram",
    )(table, items, pull, prior)

MESH = pl.DeviceIdType.MESH
routes = ("zxy", "zyx", "xzy", "yzx")


def spread_kernel(n_arc, shard, small, whole, whole_small, *sems):
    far_send, far_recv, small_send, small_recv, own_sem = sems
    arc, tile = lax.axis_index("arc"), lax.axis_index("tile")
    y, x, core = tile // 4, (tile // 2) % 2, tile % 2

    def at(y, x, core):
        return y * 4 + x * 2 + core

    links = {
        "x": (0, (arc, at(y, 1 - x, core)), None),
        "y": (1, (arc, at(1 - y, x, core)), None),
        "up": (2, (arc + 1, tile), arc + 1 < n_arc),
        "down": (3, (arc - 1, tile), arc > 0),
        "core": (4, (arc, at(y, x, 1 - core)), None),
    }

    def when(*conditions):
        conditions = [condition for condition in conditions if condition is not None]
        if not conditions:
            return lambda body: body()
        return pl.when(functools.reduce(jnp.logical_and, conditions))

    barrier = pltpu.get_barrier_semaphore()
    for _, device, there in links.values():

        @when(there)
        def _(device=device):
            pl.semaphore_signal(barrier, inc=1, device_id=device, device_id_type=MESH)

    pl.semaphore_wait(
        barrier, 3 + (arc + 1 < n_arc).astype(jnp.int32) + (arc > 0).astype(jnp.int32)
    )

    me = arc * 8 + tile
    keep = [
        pltpu.make_async_copy(shard, whole.at[me], own_sem.at[0]),
        pltpu.make_async_copy(small, whole_small.at[me], own_sem.at[1]),
    ]
    for copy in keep:
        copy.start()

    share = shard.shape[0] // len(routes)

    def copies(route, far, link, own=False, other=False):
        far_x, far_y, far_z = far
        from_y = 1 - y if far_y else y
        from_x = 1 - x if far_x else x
        chip = (arc + far_z) * 4 + from_y * 2 + from_x
        source = (arc + far_z) * 8 + at(from_y, from_x, 1 - core if other else core)
        number, device, _ = links[link]
        rows = pl.ds(route * share, share)
        arrive = 1 if other or link == "core" else 0
        made = [
            pltpu.make_async_remote_copy(
                src_ref=shard.at[rows] if own else whole.at[source, rows],
                dst_ref=whole.at[source, rows],
                send_sem=far_send.at[route, chip, number],
                recv_sem=far_recv.at[route, chip, arrive],
                device_id=device,
                device_id_type=MESH,
            )
        ]
        if route == 0:
            made.append(
                pltpu.make_async_remote_copy(
                    src_ref=small if own else whole_small.at[source],
                    dst_ref=whole_small.at[source],
                    send_sem=small_send.at[chip, number],
                    recv_sem=small_recv.at[chip, arrive],
                    device_id=device,
                    device_id_type=MESH,
                )
            )
        return made

    def onward(route, far):
        offsets = dict(zip("xyz", far))
        order = routes[route]
        last = max([order.index(axis) for axis in "xyz" if offsets[axis]], default=-1)
        out = []
        if last >= 0 and order[last] == "z":
            out.append("up" if far[2] < 0 else "down")
        for axis in order[last + 1 :]:
            out += ["up", "down"] if axis == "z" else [axis]
        return out + ["core"]

    offsets = [(i, j, k) for i in range(2) for j in range(2) for k in range(1 - n_arc, n_arc)]
    offsets.sort(key=lambda far: (far[0] + far[1] + abs(far[2]), far))
    sent = []
    for far in offsets:
        held = None if far[2] == 0 else (arc + far[2] >= 0 if far[2] < 0 else arc + far[2] < n_arc)

        @when(held)
        def _(far=far, own=far == (0, 0, 0)):
            for route in range(len(routes)):
                if not own:
                    for copy in copies(route, far, "x"):
                        copy.wait_recv()
                for link in onward(route, far):

                    @when(links[link][2])
                    def _(route=route, link=link):
                        for copy in copies(route, far, link, own):
                            copy.start()

    for far in offsets:
        held = None if far[2] == 0 else (arc + far[2] >= 0 if far[2] < 0 else arc + far[2] < n_arc)

        @when(held)
        def _(far=far, own=far == (0, 0, 0)):
            for route in range(len(routes)):
                for copy in copies(route, far, "core", other=True):
                    copy.wait_recv()
                for link in onward(route, far):

                    @when(links[link][2])
                    def _(route=route, link=link):
                        for copy in copies(route, far, link, own):
                            copy.wait_send()

    for copy in keep:
        copy.wait()


def spread_out(shard, small, n_arc):
    devices = n_arc * 8
    hbm = pl.BlockSpec(memory_space=pl.ANY)
    dma = pltpu.SemaphoreType.DMA
    whole, whole_small = pl.pallas_call(
        functools.partial(spread_kernel, n_arc),
        out_shape=(
            jax.ShapeDtypeStruct((devices, *shard.shape), shard.dtype),
            jax.ShapeDtypeStruct((devices, *small.shape), small.dtype),
        ),
        in_specs=[hbm, hbm],
        out_specs=(hbm, hbm),
        scratch_shapes=[
            dma((len(routes), n_arc * 4, 5)),
            dma((len(routes), n_arc * 4, 2)),
            dma((n_arc * 4, 5)),
            dma((n_arc * 4, 2)),
            dma((2,)),
        ],
        compiler_params=pltpu.CompilerParams(collective_id=0, has_side_effects=True),
        name="spread",
    )(shard, small)
    return whole.reshape(-1, *shard.shape[1:]), whole_small.reshape(-1, small.shape[1])


def item_table(ids, arc, owner, per_owner, row_groups):
    slots = jnp.arange(4, dtype=jnp.int32)
    owners = jnp.where(ids < 0, -1, ids // per_owner)

    def find(wanted):
        hit = owners == wanted
        return jnp.any(hit, axis=1), jnp.sum(jnp.where(hit, slots, 0), axis=1), jnp.sum(
            jnp.where(hit, ids - wanted * per_owner, 0), axis=1
        )

    named, slot, sub = find(owner)
    fields = [slot, jnp.where(named, sub, per_owner)]
    for group in range(row_groups):
        found, row_slot, row_sub = find(arc * row_groups + group)
        fields += [
            row_slot,
            jnp.where(named & found, group * per_owner + row_sub, row_groups * per_owner),
        ]
    return jnp.stack(fields, axis=1).reshape(-1)


def pack_slots(owner_of, n_owner, capacity):
    named = jnp.any(
        owner_of[None] == jnp.arange(n_owner, dtype=jnp.int32)[:, None, None], axis=2
    )
    rank = jnp.cumsum(named.astype(jnp.int32), axis=1) - 1
    chosen = named[:, None, :] & (
        rank[:, None, :] == jnp.arange(capacity, dtype=jnp.int32)[None, :, None]
    )
    block_ids = jnp.arange(owner_of.shape[0], dtype=jnp.int32)
    return jnp.any(chosen, axis=2), jnp.sum(jnp.where(chosen, block_ids, 0), axis=2)


def on_device(design, observed, obs_type, owner_of, sub_of, sigma_table, solution, prior):
    n_arc, n_owner = lax.axis_size("arc"), lax.axis_size("tile")
    blocks, block_rows, row_width = design.shape
    tile_width = row_width // 4
    per_owner = solution.shape[0] // tile_width
    row_groups = n_owner // n_arc
    capacity = 2 * ((4 * blocks + n_owner - 1) // n_owner)
    everyone = ("arc", "tile")
    tile_ids = owner_of * per_owner + sub_of
    by_route = n_owner == 8 and capacity >= blocks and blocks % len(routes) == 0
    if by_route:
        mine = jnp.zeros((-(-(solution.shape[0] + 4 * blocks) // 1024) * 1024,), jnp.float32)
        mine = mine.at[: solution.shape[0]].set(solution)
        mine = mine.at[solution.shape[0] : solution.shape[0] + 4 * blocks].set(
            tile_ids.reshape(-1).astype(jnp.float32)
        )
        both = lax.all_gather(mine.reshape(-1, tile_width), everyone, axis=0, tiled=True)
        both = both.reshape(n_arc * n_owner, -1, tile_width)
        whole_solution = both[:n_owner, :per_owner]
        all_ids = both[:, per_owner:].reshape(n_arc * n_owner, -1)[:, : 4 * blocks]
        all_ids = all_ids.astype(jnp.int32).reshape(-1, 4)
    else:
        whole_solution = lax.all_gather(solution, "tile", axis=0, tiled=True)
    weighted, pull = weigh(
        tile_ids.reshape(-1),
        sigma_table,
        whole_solution.reshape(-1, tile_width),
        design,
        observed,
        obs_type,
    )
    if by_route:
        items, pull = spread_out(weighted, pull, n_arc)
        tile_ids = all_ids
    else:
        gathered = everyone
        if capacity < blocks:
            live, block = pack_slots(owner_of, n_owner, capacity)
            over_tile = functools.partial(
                lax.all_to_all, axis_name="tile", split_axis=0, concat_axis=0, tiled=True
            )
            weighted = over_tile(weighted[block].reshape(-1, block_rows, row_width))
            pull = over_tile(pull[block].reshape(-1, row_width))
            tile_ids = over_tile(jnp.where(live[:, :, None], tile_ids[block], -1).reshape(-1, 4))
            gathered = "arc"
        tile_ids = lax.all_gather(tile_ids, gathered, axis=0, tiled=True)
        pull = lax.all_gather(pull, gathered, axis=0, tiled=True)
        items = lax.all_gather(weighted, gathered, axis=0, tiled=True)
    table = item_table(
        tile_ids, lax.axis_index("arc"), lax.axis_index("tile"), per_owner, row_groups
    )
    normal, gradient = gram(table, items, pull, prior, per_owner, row_groups, blocks)
    return normal, gradient.reshape(-1)


def solution(mesh):
    in_specs = (
        P(("arc", "tile"), None, None),
        P(("arc", "tile"), None),
        P(("arc", "tile"), None),
        P(("arc", "tile"), None),
        P(("arc", "tile"), None),
        P(),
        P("tile"),
        P("arc", "tile"),
    )
    out_specs = (P("arc", "tile"), P("tile"))
    return jax.shard_map(
        on_device, mesh=mesh, in_specs=in_specs, out_specs=out_specs, check_vma=False
    )
```

```python
import functools

import jax
import jax.numpy as jnp
from jax import lax
from jax.experimental import pallas as pl
from jax.experimental.pallas import tpu as pltpu
from jax.sharding import PartitionSpec as P

huber_limit = 1.345


def weigh_block(rows, touched, observed, types, sigma):
    rows = rows.astype(jnp.float32)
    residual = observed - jnp.sum(rows * touched, axis=1, keepdims=True)
    spread = jnp.zeros_like(residual)
    for code in range(sigma.shape[0]):
        spread = jnp.where(types == code, sigma[code], spread)
    scaled = jnp.abs(residual) / spread
    root_weight = jnp.sqrt(huber_limit / jnp.maximum(scaled, huber_limit)) / spread
    scaled_rows = (root_weight * rows).astype(jnp.bfloat16)
    target = (root_weight * residual).astype(jnp.bfloat16).astype(jnp.float32)
    return scaled_rows, jnp.sum(
        scaled_rows.astype(jnp.float32) * target, axis=0, keepdims=True
    )


def weigh_kernel(tile_ids, sigma, estimate, design, observed, obs_type, weighted, pull):
    for block in range(design.shape[0]):
        touched = jnp.concatenate(
            [estimate[pl.ds(tile_ids[4 * block + part], 1), :] for part in range(4)], axis=1
        )
        weighted[block], pull[block : block + 1, :] = weigh_block(
            design[block],
            touched,
            observed[:, block : block + 1],
            obs_type[:, block : block + 1],
            sigma,
        )


def weigh(tile_ids, sigma, estimate, design, observed, obs_type):
    blocks, block_rows, row_width = design.shape
    smem, vmem = pl.BlockSpec(memory_space=pltpu.SMEM), pl.BlockSpec(memory_space=pltpu.VMEM)
    return pl.pallas_call(
        weigh_kernel,
        out_shape=(
            jax.ShapeDtypeStruct(design.shape, jnp.bfloat16),
            jax.ShapeDtypeStruct((blocks, row_width), jnp.float32),
        ),
        in_specs=[smem, smem, vmem, vmem, vmem, vmem],
        out_specs=(vmem, vmem),
        compiler_params=pltpu.CompilerParams(vmem_limit_bytes=16 << 20),
        name="weigh",
    )(tile_ids, sigma, estimate, design, observed.T, obs_type.T)


def gram_kernel(row_groups, table, items, pull, prior, normal, gradient, total, grad_total, sem):
    step = pl.program_id(0)
    chunk, _, row_width = items.shape
    tile_width = row_width // 4
    kept = normal.shape[0]
    load = pltpu.make_async_copy(prior, total.at[pl.ds(0, kept)], sem)

    @pl.when(step == 0)
    def _():
        load.start()
        grad_total[...] = jnp.zeros_like(grad_total)
        load.wait()

    fields = 2 + 2 * row_groups
    for item in range(chunk):
        base = (step * chunk + item) * fields

        def lanes(entry):
            return pl.ds(pl.multiple_of(table[base + entry] * tile_width, tile_width), tile_width)

        part = lanes(0)
        sub = table[base + 1]
        column = pl.ds(
            pl.multiple_of(jnp.minimum(sub, gradient.shape[0] - 1) * tile_width, tile_width),
            tile_width,
        )
        grad_total[pl.ds(sub, 1), :] += pull[pl.ds(item, 1), part]
        left = jnp.concatenate(
            [items[item, :, lanes(2 + 2 * group)] for group in range(row_groups)], axis=1
        )
        products = lax.dot_general(
            left,
            items[item, :, part],
            (((0,), (0,)), ((), ())),
            preferred_element_type=jnp.float32,
        )
        for group in range(row_groups):
            total[lanes(3 + 2 * group), column] += products[
                group * tile_width : (group + 1) * tile_width
            ]

    @pl.when(step == pl.num_programs(0) - 1)
    def _():
        store = pltpu.make_async_copy(total.at[pl.ds(0, kept)], normal, sem)
        store.start()
        gradient[...] = grad_total[: gradient.shape[0]]
        store.wait()


def gram(table, items, pull, prior, per_owner, row_groups, chunk):
    count, block_rows, row_width = items.shape
    tile_width = row_width // 4
    kept, width = prior.shape
    padded = -(-(per_owner + 1) // 8) * 8
    return pl.pallas_call(
        functools.partial(gram_kernel, row_groups),
        grid_spec=pltpu.PrefetchScalarGridSpec(
            num_scalar_prefetch=1,
            grid=(count // chunk,),
            in_specs=[
                pl.BlockSpec((chunk, block_rows, row_width), lambda step, table: (step, 0, 0)),
                pl.BlockSpec((chunk, pull.shape[1]), lambda step, table: (step, 0)),
                pl.BlockSpec(memory_space=pl.ANY),
            ],
            out_specs=(
                pl.BlockSpec(memory_space=pl.ANY),
                pl.BlockSpec((per_owner, tile_width), lambda step, table: (0, 0)),
            ),
            scratch_shapes=[
                pltpu.VMEM((kept + tile_width, width), jnp.float32),
                pltpu.VMEM((padded, tile_width), jnp.float32),
                pltpu.SemaphoreType.DMA,
            ],
        ),
        out_shape=(
            jax.ShapeDtypeStruct(prior.shape, jnp.float32),
            jax.ShapeDtypeStruct((per_owner, tile_width), jnp.float32),
        ),
        compiler_params=pltpu.CompilerParams(
            vmem_limit_bytes=56 << 20
        ),
        name="gram",
    )(table, items, pull, prior)

MESH = pl.DeviceIdType.MESH
routes = ("zxy", "zyx", "xzy", "yzx")


def spread_kernel(
    n_arc,
    owner_of,
    sub_of,
    sigma,
    solution,
    numbers,
    design,
    observed,
    obs_type,
    whole,
    whole_small,
    estimate,
    shard,
    small,
    *sems,
):
    far_send, far_recv, small_send, small_recv, own_sem, early_send, early_recv = sems
    arc, tile = lax.axis_index("arc"), lax.axis_index("tile")
    y, x, core = tile // 4, (tile // 2) % 2, tile % 2

    def at(y, x, core):
        return y * 4 + x * 2 + core

    links = {
        "x": (0, (arc, at(y, 1 - x, core)), None),
        "y": (1, (arc, at(1 - y, x, core)), None),
        "up": (2, (arc + 1, tile), arc + 1 < n_arc),
        "down": (3, (arc - 1, tile), arc > 0),
        "core": (4, (arc, at(y, x, 1 - core)), None),
    }

    def when(*conditions):
        conditions = [condition for condition in conditions if condition is not None]
        if not conditions:
            return lambda body: body()
        return pl.when(functools.reduce(jnp.logical_and, conditions))

    barrier = pltpu.get_barrier_semaphore()
    for _, device, there in links.values():

        @when(there)
        def _(device=device):
            pl.semaphore_signal(barrier, inc=1, device_id=device, device_id_type=MESH)

    pl.semaphore_wait(
        barrier, 3 + (arc + 1 < n_arc).astype(jnp.int32) + (arc > 0).astype(jnp.int32)
    )

    me = arc * 8 + tile
    first = pltpu.make_async_copy(solution, estimate.at[tile], own_sem.at[0])
    first.start()
    first.wait()
    for stage, (link, start, length) in enumerate(
        [("core", tile, 1), ("x", tile // 2 * 2, 2), ("y", tile // 4 * 4, 4)]
    ):
        held = estimate.at[pl.ds(start, length)]
        copy = pltpu.make_async_remote_copy(
            src_ref=held,
            dst_ref=held,
            send_sem=early_send.at[stage],
            recv_sem=early_recv.at[stage],
            device_id=links[link][1],
            device_id_type=MESH,
        )
        copy.start()
        copy.wait()

    row_width = design.shape[2]
    small[:, row_width:] = numbers[...]

    def weigh_share(route):
        for block in range(route * share, (route + 1) * share):
            touched = jnp.concatenate(
                [
                    estimate[owner_of[4 * block + part], pl.ds(sub_of[4 * block + part], 1), :]
                    for part in range(4)
                ],
                axis=1,
            )
            shard[block], small[block : block + 1, :row_width] = weigh_block(
                design[block],
                touched,
                observed[:, block : block + 1],
                obs_type[:, block : block + 1],
                sigma,
            )

    share = shard.shape[0] // len(routes)

    def copies(route, far, link, own=False, other=False):
        far_x, far_y, far_z = far
        from_y = 1 - y if far_y else y
        from_x = 1 - x if far_x else x
        chip = (arc + far_z) * 4 + from_y * 2 + from_x
        source = (arc + far_z) * 8 + at(from_y, from_x, 1 - core if other else core)
        number, device, _ = links[link]
        rows = pl.ds(route * share, share)
        arrive = 1 if other or link == "core" else 0
        made = [
            pltpu.make_async_remote_copy(
                src_ref=shard.at[rows] if own else whole.at[source, rows],
                dst_ref=whole.at[source, rows],
                send_sem=far_send.at[route, chip, number],
                recv_sem=far_recv.at[route, chip, arrive],
                device_id=device,
                device_id_type=MESH,
            )
        ]
        if route == len(routes) - 1:
            made.append(
                pltpu.make_async_remote_copy(
                    src_ref=small if own else whole_small.at[source],
                    dst_ref=whole_small.at[source],
                    send_sem=small_send.at[chip, number],
                    recv_sem=small_recv.at[chip, arrive],
                    device_id=device,
                    device_id_type=MESH,
                )
            )
        return made

    def onward(route, far):
        offsets = dict(zip("xyz", far))
        order = routes[route]
        last = max([order.index(axis) for axis in "xyz" if offsets[axis]], default=-1)
        out = []
        if last >= 0 and order[last] == "z":
            out.append("up" if far[2] < 0 else "down")
        for axis in order[last + 1 :]:
            out += ["up", "down"] if axis == "z" else [axis]
        return out + ["core"]

    offsets = [(i, j, k) for i in range(2) for j in range(2) for k in range(1 - n_arc, n_arc)]
    offsets.sort(key=lambda far: (far[0] + far[1] + abs(far[2]), far))
    for far in offsets:
        held = None if far[2] == 0 else (arc + far[2] >= 0 if far[2] < 0 else arc + far[2] < n_arc)

        @when(held)
        def _(far=far, own=far == (0, 0, 0)):
            for route in range(len(routes)):
                if own:
                    weigh_share(route)
                else:
                    for copy in copies(route, far, "x"):
                        copy.wait_recv()
                for link in onward(route, far):

                    @when(links[link][2])
                    def _(route=route, link=link):
                        for copy in copies(route, far, link, own):
                            copy.start()

        if far == (0, 0, 0):
            keep = [
                pltpu.make_async_copy(shard, whole.at[me], own_sem.at[0]),
                pltpu.make_async_copy(small, whole_small.at[me], own_sem.at[1]),
            ]
            for copy in keep:
                copy.start()

    for far in offsets:
        held = None if far[2] == 0 else (arc + far[2] >= 0 if far[2] < 0 else arc + far[2] < n_arc)

        @when(held)
        def _(far=far, own=far == (0, 0, 0)):
            for route in range(len(routes)):
                for copy in copies(route, far, "core", other=True):
                    copy.wait_recv()
                for link in onward(route, far):

                    @when(links[link][2])
                    def _(route=route, link=link):
                        for copy in copies(route, far, link, own):
                            copy.wait_send()

    for copy in keep:
        copy.wait()


def spread_out(owner_of, sub_of, sigma, solution, numbers, design, observed, obs_type, n_arc):
    devices = n_arc * 8
    blocks, block_rows, row_width = design.shape
    hbm, vmem = pl.BlockSpec(memory_space=pl.ANY), pl.BlockSpec(memory_space=pltpu.VMEM)
    smem = pl.BlockSpec(memory_space=pltpu.SMEM)
    dma = pltpu.SemaphoreType.DMA
    small = (blocks, row_width + numbers.shape[1])
    whole, whole_small = pl.pallas_call(
        functools.partial(spread_kernel, n_arc),
        out_shape=(
            jax.ShapeDtypeStruct((devices, *design.shape), jnp.bfloat16),
            jax.ShapeDtypeStruct((devices, *small), jnp.float32),
        ),
        in_specs=[smem, smem, smem, vmem, vmem, vmem, vmem, vmem],
        out_specs=(hbm, hbm),
        scratch_shapes=[
            pltpu.VMEM((8, *solution.shape), jnp.float32),
            pltpu.VMEM(design.shape, jnp.bfloat16),
            pltpu.VMEM(small, jnp.float32),
            dma((len(routes), n_arc * 4, 5)),
            dma((len(routes), n_arc * 4, 2)),
            dma((n_arc * 4, 5)),
            dma((n_arc * 4, 2)),
            dma((2,)),
            dma((3,)),
            dma((3,)),
        ],
        compiler_params=pltpu.CompilerParams(
            collective_id=0, has_side_effects=True, vmem_limit_bytes=56 << 20
        ),
        name="spread",
    )(
        owner_of.reshape(-1),
        sub_of.reshape(-1),
        sigma,
        solution,
        numbers,
        design,
        observed.T,
        obs_type.T,
    )
    return whole.reshape(-1, block_rows, row_width), whole_small.reshape(-1, small[1])


def item_table(ids, arc, owner, per_owner, row_groups):
    slots = jnp.arange(4, dtype=jnp.int32)
    owners = jnp.where(ids < 0, -1, ids // per_owner)

    def find(wanted):
        hit = owners == wanted
        return jnp.any(hit, axis=1), jnp.sum(jnp.where(hit, slots, 0), axis=1), jnp.sum(
            jnp.where(hit, ids - wanted * per_owner, 0), axis=1
        )

    named, slot, sub = find(owner)
    fields = [slot, jnp.where(named, sub, per_owner)]
    for group in range(row_groups):
        found, row_slot, row_sub = find(arc * row_groups + group)
        fields += [
            row_slot,
            jnp.where(named & found, group * per_owner + row_sub, row_groups * per_owner),
        ]
    return jnp.stack(fields, axis=1).reshape(-1)


def pack_slots(owner_of, n_owner, capacity):
    named = jnp.any(
        owner_of[None] == jnp.arange(n_owner, dtype=jnp.int32)[:, None, None], axis=2
    )
    rank = jnp.cumsum(named.astype(jnp.int32), axis=1) - 1
    chosen = named[:, None, :] & (
        rank[:, None, :] == jnp.arange(capacity, dtype=jnp.int32)[None, :, None]
    )
    block_ids = jnp.arange(owner_of.shape[0], dtype=jnp.int32)
    return jnp.any(chosen, axis=2), jnp.sum(jnp.where(chosen, block_ids, 0), axis=2)


def on_device(design, observed, obs_type, owner_of, sub_of, sigma_table, solution, prior):
    n_arc, n_owner = lax.axis_size("arc"), lax.axis_size("tile")
    blocks, block_rows, row_width = design.shape
    tile_width = row_width // 4
    per_owner = solution.shape[0] // tile_width
    row_groups = n_owner // n_arc
    capacity = 2 * ((4 * blocks + n_owner - 1) // n_owner)
    everyone = ("arc", "tile")
    tile_ids = owner_of * per_owner + sub_of
    by_route = n_owner == 8 and capacity >= blocks and blocks % len(routes) == 0
    if by_route:
        numbers = jnp.pad(tile_ids.astype(jnp.float32), ((0, 0), (0, tile_width - 4)))
        items, pull = spread_out(
            owner_of,
            sub_of,
            sigma_table,
            solution.reshape(per_owner, tile_width),
            numbers,
            design,
            observed,
            obs_type,
            n_arc,
        )
        tile_ids = pull[:, row_width : row_width + 4].astype(jnp.int32)
    else:
        whole_solution = lax.all_gather(solution, "tile", axis=0, tiled=True)
        weighted, pull = weigh(
            tile_ids.reshape(-1),
            sigma_table,
            whole_solution.reshape(-1, tile_width),
            design,
            observed,
            obs_type,
        )
        gathered = everyone
        if capacity < blocks:
            live, block = pack_slots(owner_of, n_owner, capacity)
            over_tile = functools.partial(
                lax.all_to_all, axis_name="tile", split_axis=0, concat_axis=0, tiled=True
            )
            weighted = over_tile(weighted[block].reshape(-1, block_rows, row_width))
            pull = over_tile(pull[block].reshape(-1, row_width))
            tile_ids = over_tile(jnp.where(live[:, :, None], tile_ids[block], -1).reshape(-1, 4))
            gathered = "arc"
        tile_ids = lax.all_gather(tile_ids, gathered, axis=0, tiled=True)
        pull = lax.all_gather(pull, gathered, axis=0, tiled=True)
        items = lax.all_gather(weighted, gathered, axis=0, tiled=True)
    table = item_table(
        tile_ids, lax.axis_index("arc"), lax.axis_index("tile"), per_owner, row_groups
    )
    normal, gradient = gram(table, items, pull, prior, per_owner, row_groups, blocks)
    return normal, gradient.reshape(-1)


def solution(mesh):
    in_specs = (
        P(("arc", "tile"), None, None),
        P(("arc", "tile"), None),
        P(("arc", "tile"), None),
        P(("arc", "tile"), None),
        P(("arc", "tile"), None),
        P(),
        P("tile"),
        P("arc", "tile"),
    )
    out_specs = (P("arc", "tile"), P("tile"))
    return jax.shard_map(
        on_device, mesh=mesh, in_specs=in_specs, out_specs=out_specs, check_vma=False
    )
```

```python
import functools

import jax
import jax.numpy as jnp
from jax import lax
from jax.experimental import pallas as pl
from jax.experimental.pallas import tpu as pltpu
from jax.sharding import PartitionSpec as P

huber_limit = 1.345


def weigh_block(rows, touched, observed, types, sigma):
    rows = rows.astype(jnp.float32)
    residual = observed - jnp.sum(rows * touched, axis=1, keepdims=True)
    spread = jnp.zeros_like(residual)
    for code in range(sigma.shape[0]):
        spread = jnp.where(types == code, sigma[code], spread)
    scaled = jnp.abs(residual) / spread
    root_weight = jnp.sqrt(huber_limit / jnp.maximum(scaled, huber_limit)) / spread
    scaled_rows = (root_weight * rows).astype(jnp.bfloat16)
    target = (root_weight * residual).astype(jnp.bfloat16).astype(jnp.float32)
    return scaled_rows, jnp.sum(
        scaled_rows.astype(jnp.float32) * target, axis=0, keepdims=True
    )


def weigh_kernel(tile_ids, sigma, estimate, design, observed, obs_type, weighted, pull):
    for block in range(design.shape[0]):
        touched = jnp.concatenate(
            [estimate[pl.ds(tile_ids[4 * block + part], 1), :] for part in range(4)], axis=1
        )
        weighted[block], pull[block : block + 1, :] = weigh_block(
            design[block],
            touched,
            observed[:, block : block + 1],
            obs_type[:, block : block + 1],
            sigma,
        )


def weigh(tile_ids, sigma, estimate, design, observed, obs_type):
    blocks, block_rows, row_width = design.shape
    smem, vmem = pl.BlockSpec(memory_space=pltpu.SMEM), pl.BlockSpec(memory_space=pltpu.VMEM)
    return pl.pallas_call(
        weigh_kernel,
        out_shape=(
            jax.ShapeDtypeStruct(design.shape, jnp.bfloat16),
            jax.ShapeDtypeStruct((blocks, row_width), jnp.float32),
        ),
        in_specs=[smem, smem, vmem, vmem, vmem, vmem],
        out_specs=(vmem, vmem),
        compiler_params=pltpu.CompilerParams(vmem_limit_bytes=16 << 20),
        name="weigh",
    )(tile_ids, sigma, estimate, design, observed.T, obs_type.T)


def gram_kernel(row_groups, table, items, pull, prior, normal, gradient, total, grad_total, sem):
    step = pl.program_id(0)
    chunk, _, row_width = items.shape
    tile_width = row_width // 4
    kept = normal.shape[0]
    load = pltpu.make_async_copy(prior, total.at[pl.ds(0, kept)], sem)

    @pl.when(step == 0)
    def _():
        load.start()
        grad_total[...] = jnp.zeros_like(grad_total)
        load.wait()

    fields = 2 + 2 * row_groups
    for item in range(chunk):
        base = (step * chunk + item) * fields

        def lanes(entry):
            return pl.ds(pl.multiple_of(table[base + entry] * tile_width, tile_width), tile_width)

        part = lanes(0)
        sub = table[base + 1]
        column = pl.ds(
            pl.multiple_of(jnp.minimum(sub, gradient.shape[0] - 1) * tile_width, tile_width),
            tile_width,
        )
        grad_total[pl.ds(sub, 1), :] += pull[pl.ds(item, 1), part]
        left = jnp.concatenate(
            [items[item, :, lanes(2 + 2 * group)] for group in range(row_groups)], axis=1
        )
        products = lax.dot_general(
            left,
            items[item, :, part],
            (((0,), (0,)), ((), ())),
            preferred_element_type=jnp.float32,
        )
        for group in range(row_groups):
            total[lanes(3 + 2 * group), column] += products[
                group * tile_width : (group + 1) * tile_width
            ]

    @pl.when(step == pl.num_programs(0) - 1)
    def _():
        store = pltpu.make_async_copy(total.at[pl.ds(0, kept)], normal, sem)
        store.start()
        gradient[...] = grad_total[: gradient.shape[0]]
        store.wait()


def gram(table, items, pull, prior, per_owner, row_groups, chunk):
    count, block_rows, row_width = items.shape
    tile_width = row_width // 4
    kept, width = prior.shape
    padded = -(-(per_owner + 1) // 8) * 8
    return pl.pallas_call(
        functools.partial(gram_kernel, row_groups),
        grid_spec=pltpu.PrefetchScalarGridSpec(
            num_scalar_prefetch=1,
            grid=(count // chunk,),
            in_specs=[
                pl.BlockSpec((chunk, block_rows, row_width), lambda step, table: (step, 0, 0)),
                pl.BlockSpec((chunk, pull.shape[1]), lambda step, table: (step, 0)),
                pl.BlockSpec(memory_space=pl.ANY),
            ],
            out_specs=(
                pl.BlockSpec(memory_space=pl.ANY),
                pl.BlockSpec((per_owner, tile_width), lambda step, table: (0, 0)),
            ),
            scratch_shapes=[
                pltpu.VMEM((kept + tile_width, width), jnp.float32),
                pltpu.VMEM((padded, tile_width), jnp.float32),
                pltpu.SemaphoreType.DMA,
            ],
        ),
        out_shape=(
            jax.ShapeDtypeStruct(prior.shape, jnp.float32),
            jax.ShapeDtypeStruct((per_owner, tile_width), jnp.float32),
        ),
        compiler_params=pltpu.CompilerParams(
            vmem_limit_bytes=56 << 20
        ),
        name="gram",
    )(table, items, pull, prior)

MESH = pl.DeviceIdType.MESH
routes = ("zxy", "zyx", "xzy", "yzx")
shares = (3, 3, 5, 5)


def spread_kernel(
    n_arc,
    owner_of,
    sub_of,
    sigma,
    solution,
    design,
    observed,
    obs_type,
    whole,
    whole_small,
    estimate,
    shard,
    small,
    *sems,
):
    far_send, far_recv, small_send, small_recv, own_sem, early_send, early_recv = sems
    arc, tile = lax.axis_index("arc"), lax.axis_index("tile")
    y, x, core = tile // 4, (tile // 2) % 2, tile % 2

    def at(y, x, core):
        return y * 4 + x * 2 + core

    links = {
        "x": (0, (arc, at(y, 1 - x, core)), None),
        "y": (1, (arc, at(1 - y, x, core)), None),
        "up": (2, (arc + 1, tile), arc + 1 < n_arc),
        "down": (3, (arc - 1, tile), arc > 0),
        "core": (4, (arc, at(y, x, 1 - core)), None),
    }

    def when(*conditions):
        conditions = [condition for condition in conditions if condition is not None]
        if not conditions:
            return lambda body: body()
        return pl.when(functools.reduce(jnp.logical_and, conditions))

    barrier = pltpu.get_barrier_semaphore()
    for _, device, there in links.values():

        @when(there)
        def _(device=device):
            pl.semaphore_signal(barrier, inc=1, device_id=device, device_id_type=MESH)

    pl.semaphore_wait(
        barrier, 3 + (arc + 1 < n_arc).astype(jnp.int32) + (arc > 0).astype(jnp.int32)
    )

    me = arc * 8 + tile
    first = pltpu.make_async_copy(solution, estimate.at[tile], own_sem.at[0])
    first.start()
    first.wait()
    for stage, (link, start, length) in enumerate(
        [("core", tile, 1), ("x", tile // 2 * 2, 2), ("y", tile // 4 * 4, 4)]
    ):
        held = estimate.at[pl.ds(start, length)]
        copy = pltpu.make_async_remote_copy(
            src_ref=held,
            dst_ref=held,
            send_sem=early_send.at[stage],
            recv_sem=early_recv.at[stage],
            device_id=links[link][1],
            device_id_type=MESH,
        )
        copy.start()
        copy.wait()

    _, block_rows, row_width = design.shape
    per_owner, tile_width = estimate.shape[1:]
    lane = lax.broadcasted_iota(jnp.int32, (1, tile_width), 1)
    diagonal = lax.broadcasted_iota(
        jnp.int32, (block_rows, block_rows), 0
    ) == lax.broadcasted_iota(jnp.int32, (block_rows, block_rows), 1)

    def upright(row):
        return jnp.sum(jnp.where(diagonal, row, jnp.zeros_like(row)), axis=1, keepdims=True)

    def weigh_one(block):
        owners = [owner_of[block, part] for part in range(4)]
        subs = [sub_of[block, part] for part in range(4)]
        touched = jnp.concatenate(
            [estimate[owner, pl.ds(sub, 1), :] for owner, sub in zip(owners, subs)], axis=1
        )
        numbers = jnp.zeros((1, tile_width), jnp.int32)
        for part in range(4):
            numbers = jnp.where(lane == part, owners[part] * per_owner + subs[part], numbers)
        small[block : block + 1, row_width:] = numbers.astype(jnp.float32)
        types = upright(obs_type[block : block + 1, :].astype(jnp.float32)).astype(jnp.int32)
        rows, small[block : block + 1, :row_width] = weigh_block(
            design[block], touched, upright(observed[block : block + 1, :]), types, sigma
        )
        shard[block * block_rows : (block + 1) * block_rows, :] = rows

    unit = shard.shape[0] // sum(shares)
    starts = [unit * sum(shares[:route]) for route in range(len(routes) + 1)]

    def copies(route, far, link, own=False, other=False):
        far_x, far_y, far_z = far
        from_y = 1 - y if far_y else y
        from_x = 1 - x if far_x else x
        chip = (arc + far_z) * 4 + from_y * 2 + from_x
        source = (arc + far_z) * 8 + at(from_y, from_x, 1 - core if other else core)
        number, device, _ = links[link]
        rows = pl.ds(starts[route], starts[route + 1] - starts[route])
        arrive = 1 if other or link == "core" else 0
        made = [
            pltpu.make_async_remote_copy(
                src_ref=shard.at[rows] if own else whole.at[source, rows],
                dst_ref=whole.at[source, rows],
                send_sem=far_send.at[route, chip, number],
                recv_sem=far_recv.at[route, chip, arrive],
                device_id=device,
                device_id_type=MESH,
            )
        ]
        if route == len(routes) - 1:
            made.append(
                pltpu.make_async_remote_copy(
                    src_ref=small if own else whole_small.at[source],
                    dst_ref=whole_small.at[source],
                    send_sem=small_send.at[chip, number],
                    recv_sem=small_recv.at[chip, arrive],
                    device_id=device,
                    device_id_type=MESH,
                )
            )
        return made

    def onward(route, far):
        offsets = dict(zip("xyz", far))
        order = routes[route]
        last = max([order.index(axis) for axis in "xyz" if offsets[axis]], default=-1)
        out = []
        if last >= 0 and order[last] == "z":
            out.append("up" if far[2] < 0 else "down")
        for axis in order[last + 1 :]:
            out += ["up", "down"] if axis == "z" else [axis]
        return out + ["core"]

    offsets = [(i, j, k) for i in range(2) for j in range(2) for k in range(1 - n_arc, n_arc)]
    offsets.sort(key=lambda far: (far[0] + far[1] + abs(far[2]), far))
    for far in offsets:
        held = None if far[2] == 0 else (arc + far[2] >= 0 if far[2] < 0 else arc + far[2] < n_arc)

        @when(held)
        def _(far=far, own=far == (0, 0, 0)):
            for route in range(len(routes)):
                if own:
                    for block in range(
                        -(-starts[route] // block_rows), -(-starts[route + 1] // block_rows)
                    ):
                        weigh_one(block)
                else:
                    for copy in copies(route, far, "x"):
                        copy.wait_recv()
                for link in onward(route, far):

                    @when(links[link][2])
                    def _(route=route, link=link):
                        for copy in copies(route, far, link, own):
                            copy.start()

        if far == (0, 0, 0):
            keep = [
                pltpu.make_async_copy(shard, whole.at[me], own_sem.at[0]),
                pltpu.make_async_copy(small, whole_small.at[me], own_sem.at[1]),
            ]
            for copy in keep:
                copy.start()

    for far in offsets:
        held = None if far[2] == 0 else (arc + far[2] >= 0 if far[2] < 0 else arc + far[2] < n_arc)

        @when(held)
        def _(far=far, own=far == (0, 0, 0)):
            for route in range(len(routes)):
                for copy in copies(route, far, "core", other=True):
                    copy.wait_recv()
                for link in onward(route, far):

                    @when(links[link][2])
                    def _(route=route, link=link):
                        for copy in copies(route, far, link, own):
                            copy.wait_send()

    for copy in keep:
        copy.wait()


def spread_out(owner_of, sub_of, sigma, solution, design, observed, obs_type, n_arc):
    devices = n_arc * 8
    blocks, block_rows, row_width = design.shape
    hbm, vmem = pl.BlockSpec(memory_space=pl.ANY), pl.BlockSpec(memory_space=pltpu.VMEM)
    smem = pl.BlockSpec(memory_space=pltpu.SMEM)
    dma = pltpu.SemaphoreType.DMA
    shard = (blocks * block_rows, row_width)
    small = (blocks, row_width + solution.shape[1])
    whole, whole_small = pl.pallas_call(
        functools.partial(spread_kernel, n_arc),
        out_shape=(
            jax.ShapeDtypeStruct((devices, *shard), jnp.bfloat16),
            jax.ShapeDtypeStruct((devices, *small), jnp.float32),
        ),
        in_specs=[smem, smem, smem, vmem, vmem, vmem, vmem],
        out_specs=(hbm, hbm),
        scratch_shapes=[
            pltpu.VMEM((8, *solution.shape), jnp.float32),
            pltpu.VMEM(shard, jnp.bfloat16),
            pltpu.VMEM(small, jnp.float32),
            dma((len(routes), n_arc * 4, 5)),
            dma((len(routes), n_arc * 4, 2)),
            dma((n_arc * 4, 5)),
            dma((n_arc * 4, 2)),
            dma((2,)),
            dma((3,)),
            dma((3,)),
        ],
        compiler_params=pltpu.CompilerParams(
            collective_id=0, has_side_effects=True, vmem_limit_bytes=56 << 20
        ),
        name="spread",
    )(owner_of, sub_of, sigma, solution, design, observed, obs_type)
    return whole.reshape(-1, block_rows, row_width), whole_small.reshape(-1, small[1])


def item_table(ids, arc, owner, per_owner, row_groups):
    slots = jnp.arange(4, dtype=jnp.int32)
    owners = jnp.where(ids < 0, -1, ids // per_owner)

    def find(wanted):
        hit = owners == wanted
        return jnp.any(hit, axis=1), jnp.sum(jnp.where(hit, slots, 0), axis=1), jnp.sum(
            jnp.where(hit, ids - wanted * per_owner, 0), axis=1
        )

    named, slot, sub = find(owner)
    fields = [slot, jnp.where(named, sub, per_owner)]
    for group in range(row_groups):
        found, row_slot, row_sub = find(arc * row_groups + group)
        fields += [
            row_slot,
            jnp.where(named & found, group * per_owner + row_sub, row_groups * per_owner),
        ]
    return jnp.stack(fields, axis=1).reshape(-1)


def pack_slots(owner_of, n_owner, capacity):
    named = jnp.any(
        owner_of[None] == jnp.arange(n_owner, dtype=jnp.int32)[:, None, None], axis=2
    )
    rank = jnp.cumsum(named.astype(jnp.int32), axis=1) - 1
    chosen = named[:, None, :] & (
        rank[:, None, :] == jnp.arange(capacity, dtype=jnp.int32)[None, :, None]
    )
    block_ids = jnp.arange(owner_of.shape[0], dtype=jnp.int32)
    return jnp.any(chosen, axis=2), jnp.sum(jnp.where(chosen, block_ids, 0), axis=2)


def on_device(design, observed, obs_type, owner_of, sub_of, sigma_table, solution, prior):
    n_arc, n_owner = lax.axis_size("arc"), lax.axis_size("tile")
    blocks, block_rows, row_width = design.shape
    tile_width = row_width // 4
    per_owner = solution.shape[0] // tile_width
    row_groups = n_owner // n_arc
    capacity = 2 * ((4 * blocks + n_owner - 1) // n_owner)
    everyone = ("arc", "tile")
    tile_ids = owner_of * per_owner + sub_of
    by_route = n_owner == 8 and capacity >= blocks and blocks * block_rows % 256 == 0
    if by_route:
        items, pull = spread_out(
            owner_of,
            sub_of,
            sigma_table,
            solution.reshape(per_owner, tile_width),
            design,
            observed,
            obs_type,
            n_arc,
        )
        tile_ids = pull[:, row_width : row_width + 4].astype(jnp.int32)
    else:
        whole_solution = lax.all_gather(solution, "tile", axis=0, tiled=True)
        weighted, pull = weigh(
            tile_ids.reshape(-1),
            sigma_table,
            whole_solution.reshape(-1, tile_width),
            design,
            observed,
            obs_type,
        )
        gathered = everyone
        if capacity < blocks:
            live, block = pack_slots(owner_of, n_owner, capacity)
            over_tile = functools.partial(
                lax.all_to_all, axis_name="tile", split_axis=0, concat_axis=0, tiled=True
            )
            weighted = over_tile(weighted[block].reshape(-1, block_rows, row_width))
            pull = over_tile(pull[block].reshape(-1, row_width))
            tile_ids = over_tile(jnp.where(live[:, :, None], tile_ids[block], -1).reshape(-1, 4))
            gathered = "arc"
        tile_ids = lax.all_gather(tile_ids, gathered, axis=0, tiled=True)
        pull = lax.all_gather(pull, gathered, axis=0, tiled=True)
        items = lax.all_gather(weighted, gathered, axis=0, tiled=True)
    table = item_table(
        tile_ids, lax.axis_index("arc"), lax.axis_index("tile"), per_owner, row_groups
    )
    normal, gradient = gram(table, items, pull, prior, per_owner, row_groups, blocks)
    return normal, gradient.reshape(-1)


def solution(mesh):
    in_specs = (
        P(("arc", "tile"), None, None),
        P(("arc", "tile"), None),
        P(("arc", "tile"), None),
        P(("arc", "tile"), None),
        P(("arc", "tile"), None),
        P(),
        P("tile"),
        P("arc", "tile"),
    )
    out_specs = (P("arc", "tile"), P("tile"))
    return jax.shard_map(
        on_device, mesh=mesh, in_specs=in_specs, out_specs=out_specs, check_vma=False
    )
```

```python
import functools

import jax
import jax.numpy as jnp
from jax import lax
from jax.experimental import pallas as pl
from jax.experimental.pallas import tpu as pltpu
from jax.sharding import PartitionSpec as P

huber_limit = 1.345


def weigh_block(rows, touched, observed, types, sigma):
    rows = rows.astype(jnp.float32)
    residual = observed - jnp.sum(rows * touched, axis=1, keepdims=True)
    spread = jnp.zeros_like(residual)
    for code in range(sigma.shape[0]):
        spread = jnp.where(types == code, sigma[code], spread)
    scaled = jnp.abs(residual) / spread
    root_weight = jnp.sqrt(huber_limit / jnp.maximum(scaled, huber_limit)) / spread
    scaled_rows = (root_weight * rows).astype(jnp.bfloat16)
    target = (root_weight * residual).astype(jnp.bfloat16).astype(jnp.float32)
    return scaled_rows, jnp.sum(
        scaled_rows.astype(jnp.float32) * target, axis=0, keepdims=True
    )


def weigh_kernel(tile_ids, sigma, estimate, design, observed, obs_type, weighted, pull):
    for block in range(design.shape[0]):
        touched = jnp.concatenate(
            [estimate[pl.ds(tile_ids[4 * block + part], 1), :] for part in range(4)], axis=1
        )
        weighted[block], pull[block : block + 1, :] = weigh_block(
            design[block],
            touched,
            observed[:, block : block + 1],
            obs_type[:, block : block + 1],
            sigma,
        )


def weigh(tile_ids, sigma, estimate, design, observed, obs_type):
    blocks, block_rows, row_width = design.shape
    smem, vmem = pl.BlockSpec(memory_space=pltpu.SMEM), pl.BlockSpec(memory_space=pltpu.VMEM)
    return pl.pallas_call(
        weigh_kernel,
        out_shape=(
            jax.ShapeDtypeStruct(design.shape, jnp.bfloat16),
            jax.ShapeDtypeStruct((blocks, row_width), jnp.float32),
        ),
        in_specs=[smem, smem, vmem, vmem, vmem, vmem],
        out_specs=(vmem, vmem),
        compiler_params=pltpu.CompilerParams(vmem_limit_bytes=16 << 20),
        name="weigh",
    )(tile_ids, sigma, estimate, design, observed.T, obs_type.T)


def gram_kernel(
    row_groups, table, items, pull, prior, normal, gradient, total, grad_total, before, load_sem, sems
):
    step = pl.program_id(0)
    chunk, _, row_width = items.shape
    tile_width = row_width // 4
    kept = normal.shape[0]
    load = pltpu.make_async_copy(prior, before, load_sem)

    def slab(index):
        return pl.ds(pl.multiple_of(index * tile_width, tile_width), tile_width)

    def store(index):
        return pltpu.make_async_copy(
            total.at[slab(index)], normal.at[slab(index)], sems.at[index]
        )

    @pl.when(step == 0)
    def _():
        load.start()
        grad_total[...] = jnp.zeros_like(grad_total)

        @pl.loop(0, kept // tile_width)
        def _(index):
            total[slab(index), :] = jnp.zeros((tile_width, total.shape[1]), jnp.float32)


    fields = 2 + 2 * row_groups
    for item in range(chunk):
        base = (step * chunk + item) * fields

        def lanes(entry):
            return pl.ds(pl.multiple_of(table[base + entry] * tile_width, tile_width), tile_width)

        part = lanes(0)
        sub = table[base + 1]
        column = pl.ds(
            pl.multiple_of(jnp.minimum(sub, gradient.shape[0] - 1) * tile_width, tile_width),
            tile_width,
        )
        grad_total[pl.ds(sub, 1), :] += pull[pl.ds(item, 1), part]
        left = jnp.concatenate(
            [items[item, :, lanes(2 + 2 * group)] for group in range(row_groups)], axis=1
        )
        products = lax.dot_general(
            left,
            items[item, :, part],
            (((0,), (0,)), ((), ())),
            preferred_element_type=jnp.float32,
        )
        for group in range(row_groups):
            total[lanes(3 + 2 * group), column] += products[
                group * tile_width : (group + 1) * tile_width
            ]

    @pl.when(step == pl.num_programs(0) - 1)
    def _():
        load.wait()

        @pl.loop(0, kept // tile_width)
        def _(index):
            total[slab(index), :] += before[slab(index), :]
            store(index).start()

        gradient[...] = grad_total[: gradient.shape[0]]

        @pl.loop(0, kept // tile_width)
        def _(index):
            store(index).wait()


def gram(table, items, pull, prior, per_owner, row_groups, chunk):
    count, block_rows, row_width = items.shape
    tile_width = row_width // 4
    kept, width = prior.shape
    padded = -(-(per_owner + 1) // 8) * 8
    return pl.pallas_call(
        functools.partial(gram_kernel, row_groups),
        grid_spec=pltpu.PrefetchScalarGridSpec(
            num_scalar_prefetch=1,
            grid=(count // chunk,),
            in_specs=[
                pl.BlockSpec((chunk, block_rows, row_width), lambda step, table: (step, 0, 0)),
                pl.BlockSpec((chunk, pull.shape[1]), lambda step, table: (step, 0)),
                pl.BlockSpec(memory_space=pl.ANY),
            ],
            out_specs=(
                pl.BlockSpec(memory_space=pl.ANY),
                pl.BlockSpec((per_owner, tile_width), lambda step, table: (0, 0)),
            ),
            scratch_shapes=[
                pltpu.VMEM((kept + tile_width, width), jnp.float32),
                pltpu.VMEM((padded, tile_width), jnp.float32),
                pltpu.VMEM(prior.shape, jnp.float32),
                pltpu.SemaphoreType.DMA,
                pltpu.SemaphoreType.DMA((kept // tile_width,)),
            ],
        ),
        out_shape=(
            jax.ShapeDtypeStruct(prior.shape, jnp.float32),
            jax.ShapeDtypeStruct((per_owner, tile_width), jnp.float32),
        ),
        compiler_params=pltpu.CompilerParams(
            vmem_limit_bytes=56 << 20
        ),
        name="gram",
    )(table, items, pull, prior)

MESH = pl.DeviceIdType.MESH
routes = ("zxy", "zyx", "xzy", "yzx")
shares = (3, 3, 5, 5)


def spread_kernel(
    n_arc,
    owner_of,
    sub_of,
    sigma,
    solution,
    design,
    observed,
    obs_type,
    whole,
    whole_small,
    estimate,
    shard,
    small,
    *sems,
):
    far_send, far_recv, small_send, small_recv, own_sem, early_send, early_recv = sems
    arc, tile = lax.axis_index("arc"), lax.axis_index("tile")
    y, x, core = tile // 4, (tile // 2) % 2, tile % 2

    def at(y, x, core):
        return y * 4 + x * 2 + core

    links = {
        "x": (0, (arc, at(y, 1 - x, core)), None),
        "y": (1, (arc, at(1 - y, x, core)), None),
        "up": (2, (arc + 1, tile), arc + 1 < n_arc),
        "down": (3, (arc - 1, tile), arc > 0),
        "core": (4, (arc, at(y, x, 1 - core)), None),
    }

    def when(*conditions):
        conditions = [condition for condition in conditions if condition is not None]
        if not conditions:
            return lambda body: body()
        return pl.when(functools.reduce(jnp.logical_and, conditions))

    barrier = pltpu.get_barrier_semaphore()
    for _, device, there in links.values():

        @when(there)
        def _(device=device):
            pl.semaphore_signal(barrier, inc=1, device_id=device, device_id_type=MESH)

    pl.semaphore_wait(
        barrier, 3 + (arc + 1 < n_arc).astype(jnp.int32) + (arc > 0).astype(jnp.int32)
    )

    me = arc * 8 + tile
    first = pltpu.make_async_copy(solution, estimate.at[tile], own_sem.at[0])
    first.start()
    first.wait()
    for stage, (link, start, length) in enumerate(
        [("core", tile, 1), ("x", tile // 2 * 2, 2), ("y", tile // 4 * 4, 4)]
    ):
        held = estimate.at[pl.ds(start, length)]
        copy = pltpu.make_async_remote_copy(
            src_ref=held,
            dst_ref=held,
            send_sem=early_send.at[stage],
            recv_sem=early_recv.at[stage],
            device_id=links[link][1],
            device_id_type=MESH,
        )
        copy.start()
        copy.wait()

    _, block_rows, row_width = design.shape
    per_owner, tile_width = estimate.shape[1:]
    lane = lax.broadcasted_iota(jnp.int32, (1, tile_width), 1)
    diagonal = lax.broadcasted_iota(
        jnp.int32, (block_rows, block_rows), 0
    ) == lax.broadcasted_iota(jnp.int32, (block_rows, block_rows), 1)

    def upright(row):
        return jnp.sum(jnp.where(diagonal, row, jnp.zeros_like(row)), axis=1, keepdims=True)

    def weigh_one(block):
        owners = [owner_of[block, part] for part in range(4)]
        subs = [sub_of[block, part] for part in range(4)]
        touched = jnp.concatenate(
            [estimate[owner, pl.ds(sub, 1), :] for owner, sub in zip(owners, subs)], axis=1
        )
        numbers = jnp.zeros((1, tile_width), jnp.int32)
        for part in range(4):
            numbers = jnp.where(lane == part, owners[part] * per_owner + subs[part], numbers)
        small[block : block + 1, row_width:] = numbers.astype(jnp.float32)
        types = upright(obs_type[block : block + 1, :].astype(jnp.float32)).astype(jnp.int32)
        rows, small[block : block + 1, :row_width] = weigh_block(
            design[block], touched, upright(observed[block : block + 1, :]), types, sigma
        )
        shard[block * block_rows : (block + 1) * block_rows, :] = rows

    unit = shard.shape[0] // sum(shares)
    starts = [unit * sum(shares[:route]) for route in range(len(routes) + 1)]

    def copies(route, far, link, own=False, other=False):
        far_x, far_y, far_z = far
        from_y = 1 - y if far_y else y
        from_x = 1 - x if far_x else x
        chip = (arc + far_z) * 4 + from_y * 2 + from_x
        source = (arc + far_z) * 8 + at(from_y, from_x, 1 - core if other else core)
        number, device, _ = links[link]
        rows = pl.ds(starts[route], starts[route + 1] - starts[route])
        arrive = 1 if other or link == "core" else 0
        made = [
            pltpu.make_async_remote_copy(
                src_ref=shard.at[rows] if own else whole.at[source, rows],
                dst_ref=whole.at[source, rows],
                send_sem=far_send.at[route, chip, number],
                recv_sem=far_recv.at[route, chip, arrive],
                device_id=device,
                device_id_type=MESH,
            )
        ]
        if route == len(routes) - 1:
            made.append(
                pltpu.make_async_remote_copy(
                    src_ref=small if own else whole_small.at[source],
                    dst_ref=whole_small.at[source],
                    send_sem=small_send.at[chip, number],
                    recv_sem=small_recv.at[chip, arrive],
                    device_id=device,
                    device_id_type=MESH,
                )
            )
        return made

    def onward(route, far):
        offsets = dict(zip("xyz", far))
        order = routes[route]
        last = max([order.index(axis) for axis in "xyz" if offsets[axis]], default=-1)
        out = []
        if last >= 0 and order[last] == "z":
            out.append("up" if far[2] < 0 else "down")
        for axis in order[last + 1 :]:
            out += ["up", "down"] if axis == "z" else [axis]
        return out + ["core"]

    offsets = [(i, j, k) for i in range(2) for j in range(2) for k in range(1 - n_arc, n_arc)]
    offsets.sort(key=lambda far: (far[0] + far[1] + abs(far[2]), far))
    for far in offsets:
        held = None if far[2] == 0 else (arc + far[2] >= 0 if far[2] < 0 else arc + far[2] < n_arc)

        @when(held)
        def _(far=far, own=far == (0, 0, 0)):
            for route in range(len(routes)):
                if own:
                    for block in range(
                        -(-starts[route] // block_rows), -(-starts[route + 1] // block_rows)
                    ):
                        weigh_one(block)
                else:
                    for copy in copies(route, far, "x"):
                        copy.wait_recv()
                for link in onward(route, far):

                    @when(links[link][2])
                    def _(route=route, link=link):
                        for copy in copies(route, far, link, own):
                            copy.start()

        if far == (0, 0, 0):
            keep = [
                pltpu.make_async_copy(shard, whole.at[me], own_sem.at[0]),
                pltpu.make_async_copy(small, whole_small.at[me], own_sem.at[1]),
            ]
            for copy in keep:
                copy.start()

    for far in offsets:
        held = None if far[2] == 0 else (arc + far[2] >= 0 if far[2] < 0 else arc + far[2] < n_arc)

        @when(held)
        def _(far=far, own=far == (0, 0, 0)):
            for route in range(len(routes)):
                for copy in copies(route, far, "core", other=True):
                    copy.wait_recv()
                for link in onward(route, far):

                    @when(links[link][2])
                    def _(route=route, link=link):
                        for copy in copies(route, far, link, own):
                            copy.wait_send()

    for copy in keep:
        copy.wait()


def spread_out(owner_of, sub_of, sigma, solution, design, observed, obs_type, n_arc):
    devices = n_arc * 8
    blocks, block_rows, row_width = design.shape
    hbm, vmem = pl.BlockSpec(memory_space=pl.ANY), pl.BlockSpec(memory_space=pltpu.VMEM)
    smem = pl.BlockSpec(memory_space=pltpu.SMEM)
    dma = pltpu.SemaphoreType.DMA
    shard = (blocks * block_rows, row_width)
    small = (blocks, row_width + solution.shape[1])
    whole, whole_small = pl.pallas_call(
        functools.partial(spread_kernel, n_arc),
        out_shape=(
            jax.ShapeDtypeStruct((devices, *shard), jnp.bfloat16),
            jax.ShapeDtypeStruct((devices, *small), jnp.float32),
        ),
        in_specs=[smem, smem, smem, vmem, vmem, vmem, vmem],
        out_specs=(hbm, hbm),
        scratch_shapes=[
            pltpu.VMEM((8, *solution.shape), jnp.float32),
            pltpu.VMEM(shard, jnp.bfloat16),
            pltpu.VMEM(small, jnp.float32),
            dma((len(routes), n_arc * 4, 5)),
            dma((len(routes), n_arc * 4, 2)),
            dma((n_arc * 4, 5)),
            dma((n_arc * 4, 2)),
            dma((2,)),
            dma((3,)),
            dma((3,)),
        ],
        compiler_params=pltpu.CompilerParams(
            collective_id=0, has_side_effects=True, vmem_limit_bytes=56 << 20
        ),
        name="spread",
    )(owner_of, sub_of, sigma, solution, design, observed, obs_type)
    return whole.reshape(-1, block_rows, row_width), whole_small.reshape(-1, small[1])


def item_table(ids, arc, owner, per_owner, row_groups):
    slots = jnp.arange(4, dtype=jnp.int32)
    owners = jnp.where(ids < 0, -1, ids // per_owner)

    def find(wanted):
        hit = owners == wanted
        return jnp.any(hit, axis=1), jnp.sum(jnp.where(hit, slots, 0), axis=1), jnp.sum(
            jnp.where(hit, ids - wanted * per_owner, 0), axis=1
        )

    named, slot, sub = find(owner)
    fields = [slot, jnp.where(named, sub, per_owner)]
    for group in range(row_groups):
        found, row_slot, row_sub = find(arc * row_groups + group)
        fields += [
            row_slot,
            jnp.where(named & found, group * per_owner + row_sub, row_groups * per_owner),
        ]
    return jnp.stack(fields, axis=1).reshape(-1)


def pack_slots(owner_of, n_owner, capacity):
    named = jnp.any(
        owner_of[None] == jnp.arange(n_owner, dtype=jnp.int32)[:, None, None], axis=2
    )
    rank = jnp.cumsum(named.astype(jnp.int32), axis=1) - 1
    chosen = named[:, None, :] & (
        rank[:, None, :] == jnp.arange(capacity, dtype=jnp.int32)[None, :, None]
    )
    block_ids = jnp.arange(owner_of.shape[0], dtype=jnp.int32)
    return jnp.any(chosen, axis=2), jnp.sum(jnp.where(chosen, block_ids, 0), axis=2)


def on_device(design, observed, obs_type, owner_of, sub_of, sigma_table, solution, prior):
    n_arc, n_owner = lax.axis_size("arc"), lax.axis_size("tile")
    blocks, block_rows, row_width = design.shape
    tile_width = row_width // 4
    per_owner = solution.shape[0] // tile_width
    row_groups = n_owner // n_arc
    capacity = 2 * ((4 * blocks + n_owner - 1) // n_owner)
    everyone = ("arc", "tile")
    tile_ids = owner_of * per_owner + sub_of
    by_route = n_owner == 8 and capacity >= blocks and blocks * block_rows % 256 == 0
    if by_route:
        items, pull = spread_out(
            owner_of,
            sub_of,
            sigma_table,
            solution.reshape(per_owner, tile_width),
            design,
            observed,
            obs_type,
            n_arc,
        )
        tile_ids = pull[:, row_width : row_width + 4].astype(jnp.int32)
    else:
        whole_solution = lax.all_gather(solution, "tile", axis=0, tiled=True)
        weighted, pull = weigh(
            tile_ids.reshape(-1),
            sigma_table,
            whole_solution.reshape(-1, tile_width),
            design,
            observed,
            obs_type,
        )
        gathered = everyone
        if capacity < blocks:
            live, block = pack_slots(owner_of, n_owner, capacity)
            over_tile = functools.partial(
                lax.all_to_all, axis_name="tile", split_axis=0, concat_axis=0, tiled=True
            )
            weighted = over_tile(weighted[block].reshape(-1, block_rows, row_width))
            pull = over_tile(pull[block].reshape(-1, row_width))
            tile_ids = over_tile(jnp.where(live[:, :, None], tile_ids[block], -1).reshape(-1, 4))
            gathered = "arc"
        tile_ids = lax.all_gather(tile_ids, gathered, axis=0, tiled=True)
        pull = lax.all_gather(pull, gathered, axis=0, tiled=True)
        items = lax.all_gather(weighted, gathered, axis=0, tiled=True)
    table = item_table(
        tile_ids, lax.axis_index("arc"), lax.axis_index("tile"), per_owner, row_groups
    )
    normal, gradient = gram(table, items, pull, prior, per_owner, row_groups, 2 * blocks)
    return normal, gradient.reshape(-1)


def solution(mesh):
    in_specs = (
        P(("arc", "tile"), None, None),
        P(("arc", "tile"), None),
        P(("arc", "tile"), None),
        P(("arc", "tile"), None),
        P(("arc", "tile"), None),
        P(),
        P("tile"),
        P("arc", "tile"),
    )
    out_specs = (P("arc", "tile"), P("tile"))
    return jax.shard_map(
        on_device, mesh=mesh, in_specs=in_specs, out_specs=out_specs, check_vma=False
    )
```
